32 devices in a mesh: lon: 16 (over z, y, core), lat: 2 (over x).
Axes of the slice: x: 2, y: 2, z: 4, core: 2. Of those that a mesh axis runs over, the one named last changes fastest.
Arguments:
- fine_tokens: bfloat16 [72, 384, 512], P('lat', 'lon'), may hold values from -6 to 6
- fine_qkv: bfloat16 [512, 1536], replicated, may hold values from -0.25 to 0.25
- fine_scale: float32 [8], replicated, may hold values from 3 to 15
- fine_proj: bfloat16 [512, 512], replicated, may hold values from -0.25 to 0.25
- window_mask: int32 [13, 32], replicated, may hold values from 0 to 3
- merge_weight: bfloat16 [2048, 1024], replicated, may hold values from -0.125 to 0.125
- mid_qkv: bfloat16 [1024, 1536], replicated, may hold values from -0.1875 to 0.1875
- mid_scale: float32 [8], replicated, may hold values from 3 to 15
- mid_proj: bfloat16 [512, 1024], replicated, may hold values from -0.25 to 0.25
Outputs:
- fine_out: bfloat16 [72, 384, 512], P('lat', 'lon')
- mid_out: bfloat16 [36, 192, 1024], P('lat', 'lon')
The draws below stay inside these ranges and needn't reach their ends.
Inputs may be any that keep to these rules, and one draw needn't show every extreme that they name: `window_mask`: the bit of value 1 in a window's mask splits its upper and lower halves, the bit of value 2 its western and eastern halves.
All inputs are finite; a program needn't handle non-finite values.
Results may differ from the reference program's by a relative error of at most 0.015.
Values may be sent and summed in bfloat16 or wider, within the bound.
A program may use at most 128 MiB of HBM per device.

```python
import math
import jax
import jax.numpy as jnp
from jax import lax

C1 = 512
C2 = 1024
H1 = 8
HEAD = 64
H2 = 8
WLAT = 6
WLON = 12
LAT = 72
LON = 384
NWR = 13
NWC = 32


def with_ends(values, own_key, smallest, top_value):
    longest = values.shape.index(max(values.shape))
    spots = []
    for shift in (0, 1):
        where = [jax.random.randint(jax.random.fold_in(own_key, axis), (), 0, length) for axis, length in enumerate(values.shape)]
        where[longest] = (where[longest] + shift) % values.shape[longest]
        spots.append(tuple(where))
    return values.at[spots[0]].set(smallest).at[spots[1]].set(top_value)


def levels(key, dims, split, smallest, high):
    gain = 1.0
    for dim, shards_of in split:
        steps = jax.random.uniform(jax.random.fold_in(jax.random.fold_in(key, 6), dim), (shards_of,), jnp.float32, smallest / len(split), high / len(split))
        gain = gain * jnp.repeat(jnp.exp(steps), dims[dim] // shards_of).reshape((-1,) + (1,) * (len(dims) - 1 - dim))
    return gain


def scatter_about(own_key, extent, spread, bound, pieces=(), kind=jnp.bfloat16):
    entries = spread * jax.random.normal(own_key, extent, jnp.float32)
    if pieces:
        entries = entries * levels(own_key, extent, pieces, -0.22, 0.18)
    return jnp.clip(entries, -bound, bound).astype(kind)


def setup_inputs(seed: int = 0) -> dict:
    key_list = jax.random.split(jax.random.key(seed), 10)
    return {
        "fine_tokens": scatter_about(key_list[0], (LAT, LON, C1), 1.0, 6.0, ((0, 2), (1, 16))),
        "fine_qkv": scatter_about(key_list[1], (C1, 3 * C1), C1 ** -0.5, 0.25),
        "fine_scale": jnp.clip(jnp.exp(jax.random.uniform(key_list[2], (H1,), jnp.float32, math.log(3.0), math.log(15.0))), 3.0, 15.0),
        "fine_proj": scatter_about(key_list[3], (C1, C1), C1 ** -0.5, 0.25),
        "window_mask": with_ends(jax.random.randint(key_list[4], (NWR, NWC), 0, 4), jax.random.fold_in(key_list[4], 1), 0, 3).astype(jnp.int32),
        "merge_weight": scatter_about(key_list[5], (4 * C1, C2), (4 * C1) ** -0.5, 0.125),
        "mid_qkv": scatter_about(key_list[6], (C2, 3 * H2 * HEAD), C2 ** -0.5, 0.1875),
        "mid_scale": jnp.clip(jnp.exp(jax.random.uniform(key_list[7], (H2,), jnp.float32, math.log(3.0), math.log(15.0))), 3.0, 15.0),
        "mid_proj": scatter_about(key_list[8], (H2 * HEAD, C2), (H2 * HEAD) ** -0.5, 0.25),
    }


EPS_NORM = 1e-05
EPS_DIR = 1e-06

def layer_norm(values):
    mean = lax.optimization_barrier(jnp.mean(values, axis=-1, keepdims=True))
    centred = values - mean
    var = lax.optimization_barrier(jnp.mean(centred * centred, axis=-1, keepdims=True))
    return centred * lax.rsqrt(var + EPS_NORM)

def window_attention(query, keys, values, scale, allowed):
    query_f = query.astype(jnp.float32)
    keys_f = keys.astype(jnp.float32)
    raw = jnp.einsum('wqhe,wkhe->whqk', query_f, keys_f)
    query_inv = lax.rsqrt(lax.optimization_barrier(jnp.sum(query_f * query_f, axis=-1)) + EPS_DIR)
    keys_inv = lax.rsqrt(lax.optimization_barrier(jnp.sum(keys_f * keys_f, axis=-1)) + EPS_DIR)
    cosine = raw * jnp.transpose(query_inv, (0, 2, 1))[:, :, :, None] * jnp.transpose(keys_inv, (0, 2, 1))[:, :, None, :]
    expo = jnp.where(allowed[:, None], jnp.exp(scale[None, :, None, None] * cosine), jnp.float32(0.0))
    weights = (expo / lax.optimization_barrier(jnp.sum(expo, axis=-1, keepdims=True))).astype(jnp.bfloat16)
    mixed = jnp.einsum('whqk,wkhe->wqhe', weights.astype(jnp.float32), values.astype(jnp.float32))
    return mixed.astype(jnp.bfloat16)

def reference(fine_tokens, fine_qkv, fine_scale, fine_proj, window_mask, merge_weight, mid_qkv, mid_scale, mid_proj):
    half_lat = WLAT // 2
    half_lon = WLON // 2
    padded = jnp.pad(fine_tokens, ((half_lat, half_lat), (0, 0), (0, 0)))
    padded = jnp.roll(padded, -half_lon, axis=1)
    lat_part = jnp.broadcast_to(jnp.arange(WLAT)[:, None] >= half_lat, (WLAT, WLON)).reshape(-1)
    lon_part = jnp.broadcast_to(jnp.arange(WLON)[None, :] >= half_lon, (WLAT, WLON)).reshape(-1)
    same_lat = lat_part[:, None] == lat_part[None, :]
    same_lon = lon_part[:, None] == lon_part[None, :]
    place = WLAT * WLON

    def fine_band(band):
        rows = lax.dynamic_slice_in_dim(padded, band * WLAT, WLAT, 0)
        act = jnp.dot(rows.reshape(-1, C1), fine_qkv, preferred_element_type=jnp.float32).astype(jnp.bfloat16)
        act = act.reshape(WLAT, NWC, WLON, 3, H1, HEAD).transpose(1, 0, 2, 3, 4, 5).reshape(NWC, place, 3, H1, HEAD)
        glob_row = band * WLAT - half_lat + jnp.arange(WLAT, dtype=jnp.int32)
        valid = (glob_row >= 0) & (glob_row < LAT)
        valid_key = jnp.repeat(valid, WLON)
        pattern = lax.dynamic_index_in_dim(window_mask, band, 0, keepdims=False)
        split_lat = pattern % 2 == 1
        split_lon = pattern // 2 == 1
        allowed = valid_key[None, None, :] & (jnp.logical_not(split_lat)[:, None, None] | same_lat[None]) & (jnp.logical_not(split_lon)[:, None, None] | same_lon[None])
        mixed = window_attention(act[:, :, 0], act[:, :, 1], act[:, :, 2], fine_scale, allowed)
        mixed = mixed.reshape(NWC, WLAT, WLON, C1).transpose(1, 0, 2, 3).reshape(WLAT * LON, C1)
        projected = jnp.dot(mixed, fine_proj, preferred_element_type=jnp.float32)
        result = rows.reshape(-1, C1).astype(jnp.float32) + layer_norm(projected)
        return result.astype(jnp.bfloat16).reshape(WLAT, LON, C1)
    bands = lax.map(fine_band, jnp.arange(NWR, dtype=jnp.int32))
    fine_out = bands.reshape(NWR * WLAT, LON, C1)[half_lat:half_lat + LAT]
    fine_out = jnp.roll(fine_out, half_lon, axis=1)
    quads = fine_out.reshape(LAT // 2, 2, LON // 2, 2, C1).transpose(0, 2, 3, 1, 4).reshape(LAT // 2, LON // 2, 4 * C1)
    merge_in = layer_norm(quads.astype(jnp.float32)).astype(jnp.bfloat16)
    merged = jnp.dot(merge_in.reshape(-1, 4 * C1), merge_weight, preferred_element_type=jnp.float32).astype(jnp.bfloat16)
    merged = merged.reshape(LAT // 2, LON // 2, C2)
    mid_width = H2 * HEAD
    mid_cols = LON // 2 // WLON
    every = jnp.ones((1, 1, 1), dtype=bool)

    def mid_band(band):
        rows = lax.dynamic_slice_in_dim(merged, band * WLAT, WLAT, 0)
        act = jnp.dot(rows.reshape(-1, C2), mid_qkv, preferred_element_type=jnp.float32).astype(jnp.bfloat16)
        act = act.reshape(WLAT, mid_cols, WLON, 3, H2, HEAD).transpose(1, 0, 2, 3, 4, 5).reshape(mid_cols, place, 3, H2, HEAD)
        mixed = window_attention(act[:, :, 0], act[:, :, 1], act[:, :, 2], mid_scale, every)
        mixed = mixed.reshape(mid_cols, WLAT, WLON, mid_width).transpose(1, 0, 2, 3).reshape(-1, mid_width)
        projected = jnp.dot(mixed, mid_proj, preferred_element_type=jnp.float32)
        result = rows.reshape(-1, C2).astype(jnp.float32) + layer_norm(projected)
        return result.astype(jnp.bfloat16).reshape(WLAT, LON // 2, C2)
    mid_out = lax.map(mid_band, jnp.arange(LAT // 2 // WLAT, dtype=jnp.int32)).reshape(LAT // 2, LON // 2, C2)
    return (fine_out, mid_out)
```

```python
import functools
import math

import jax
import jax.numpy as jnp
import numpy as np
from jax import lax
from jax.experimental import pallas as pl
from jax.experimental.pallas import tpu as pltpu
from jax.sharding import PartitionSpec as P

WLAT = 6
WLON = 12
HEAD = 64
TILE = 8
LANES = 128
EPS_NORM = 1e-05
EPS_DIR = 1e-06
LOG2E = math.log2(math.e)
MESH = pl.DeviceIdType.MESH
BF16 = jnp.bfloat16
F32 = jnp.float32


def exchange_kernel(lat_count, lon_count, tokens, side, latr, send_sem, recv_sem):
    rows, blocks = tokens.shape[0], tokens.shape[1]
    half = WLAT // 2
    lat, lon = lax.axis_index("lat"), lax.axis_index("lon")
    south, north = lax.rem(lat + 1, lat_count), lax.rem(lat + lat_count - 1, lat_count)
    east, west = lax.rem(lon + 1, lon_count), lax.rem(lon + lon_count - 1, lon_count)
    last = blocks - 1
    top, bottom = pl.ds(0, half), pl.ds(rows - half, half)
    ext_top, ext_bottom, middle = pl.ds(0, half), pl.ds(rows + half, half), pl.ds(half, rows)
    plan = [
        ((lat, east), tokens.at[:, last], side.at[middle, 0]),
        ((lat, west), tokens.at[:, 0], side.at[middle, 1]),
        ((south, lon), tokens.at[bottom], latr.at[0]),
        ((north, lon), tokens.at[top], latr.at[1]),
        ((south, east), tokens.at[bottom, last], side.at[ext_top, 0]),
        ((north, east), tokens.at[top, last], side.at[ext_bottom, 0]),
        ((south, west), tokens.at[bottom, 0], side.at[ext_top, 1]),
        ((north, west), tokens.at[top, 0], side.at[ext_bottom, 1]),
    ]
    barrier = pltpu.get_barrier_semaphore()
    for (to_lat, to_lon), _, _ in plan:
        pl.semaphore_signal(
            barrier, inc=1, device_id={"lat": to_lat, "lon": to_lon}, device_id_type=MESH
        )
    pl.semaphore_wait(barrier, len(plan))
    copies = []
    for n, ((to_lat, to_lon), src, dst) in enumerate(plan):
        copy = pltpu.make_async_remote_copy(
            src_ref=src,
            dst_ref=dst,
            send_sem=send_sem.at[n],
            recv_sem=recv_sem.at[n],
            device_id={"lat": to_lat, "lon": to_lon},
            device_id_type=MESH,
        )
        copy.start()
        copies.append(copy)
    for copy in copies:
        copy.wait()


def exchange(tokens, lat_count, lon_count):
    rows, _, _, width = tokens.shape
    return pl.pallas_call(
        functools.partial(exchange_kernel, lat_count, lon_count),
        out_shape=(
            jax.ShapeDtypeStruct((rows + WLAT, 2, TILE, width), BF16),
            jax.ShapeDtypeStruct((2, WLAT // 2) + tokens.shape[1:], BF16),
        ),
        in_specs=[pl.BlockSpec(memory_space=pl.ANY)],
        out_specs=(pl.BlockSpec(memory_space=pl.ANY),) * 2,
        scratch_shapes=[pltpu.SemaphoreType.DMA((8,)), pltpu.SemaphoreType.DMA((8,))],
        compiler_params=pltpu.CompilerParams(collective_id=0, has_side_effects=True),
    )(tokens)


def normed(values):
    mean = jnp.mean(values, axis=-1, keepdims=True)
    centred = values - mean
    var = jnp.mean(centred * centred, axis=-1, keepdims=True)
    return centred * lax.rsqrt(var + EPS_NORM)


def dot(a, b):
    return jnp.dot(a, b, preferred_element_type=F32)


def directions(values, ones_block, scale_row):
    held = values.astype(BF16).astype(F32)
    squares = (held * held).astype(BF16)
    block = ones_block.shape[0]
    sums = jnp.concatenate(
        [dot(squares[:, s : s + block], ones_block) for s in range(0, values.shape[1], block)],
        axis=1,
    )
    unit = held * lax.rsqrt(sums + EPS_DIR)
    if scale_row is not None:
        unit = unit * scale_row
    return unit.astype(BF16)


def scale_lanes(scale, heads):
    lane = lax.broadcasted_iota(jnp.int32, (1, LANES), 1)
    return jnp.concatenate(
        [
            jnp.where(lane < HEAD, scale[h] * LOG2E, scale[h + 1] * LOG2E)
            for h in range(0, heads, 2)
        ],
        axis=1,
    )


def attend(query, keys, values, allowed):
    count = query.shape[0]
    lane = lax.broadcasted_iota(jnp.int32, (1, LANES), 1)
    low = (lane < HEAD).astype(F32).astype(BF16)
    high = (lane >= HEAD).astype(F32).astype(BF16)
    first = jnp.broadcast_to(lane < HEAD, (count, LANES))
    ones = jnp.ones((keys.shape[0], LANES), BF16)
    both = jnp.concatenate([allowed, allowed], axis=0)
    mixed = []
    for s in range(0, query.shape[1], LANES):
        pair = query[:, s : s + LANES]
        stacked = jnp.concatenate([pair * low, pair * high], axis=0)
        score = lax.dot_general(
            stacked, keys[:, s : s + LANES], (((1,), (1,)), ((), ())), preferred_element_type=F32
        )
        expo = (jnp.exp2(score) * both).astype(BF16)
        out = dot(expo, jnp.concatenate([values[:, s : s + LANES], ones], axis=1))
        top = jnp.where(first, out[:count, :LANES], out[count:, :LANES])
        total = jnp.where(first, out[:count, LANES:], out[count:, LANES:])
        mixed.append(top / total)
    return jnp.concatenate(mixed, axis=1)


def body_kernel(
    lat_count,
    fine_scale,
    mid_scale,
    window_mask,
    q_static,
    k_static,
    mid_q,
    mid_k,
    ones_block,
    perm,
    spread,
    tokens,
    side,
    latr,
    fine_qkv,
    fine_proj,
    merge_weight,
    mid_qkv,
    mid_proj,
    fine_out,
    mid_out,
    core,
    halo,
    w_qkv,
    w_proj,
    w_merge,
    w_mqkv,
    w_mproj,
    mix,
    out_buf,
    sem,
    out_sem,
):
    rows, blocks, _, width = tokens.shape
    half = WLAT // 2
    cols = blocks * TILE
    bands = (rows + WLAT) // WLAT
    loads = [
        pltpu.make_async_copy(src, dst, sem.at[n])
        for n, (src, dst) in enumerate(
            [
                (tokens, core.at[pl.ds(half, rows)]),
                (latr.at[0], core.at[pl.ds(0, half)]),
                (latr.at[1], core.at[pl.ds(rows + half, half)]),
                (side, halo),
                (fine_qkv, w_qkv),
                (fine_proj, w_proj),
                (merge_weight, w_merge),
                (mid_qkv, w_mqkv),
                (mid_proj, w_mproj),
            ]
        )
    ]
    for load in loads:
        load.start()
    lat, lon = lax.axis_index("lat"), lax.axis_index("lon")
    fine_row = scale_lanes(fine_scale, width // HEAD)
    q_win, q_lat, q_lon = q_static[:, 0:1], q_static[:, 1:2], q_static[:, 2:3]
    k_win, k_lat, k_lon = k_static[0:1], k_static[1:2], k_static[2:3]
    per_row = window_mask.shape[1]
    blocks_of = ones_block[...]
    for load in loads[:5]:
        load.wait()

    def band_step(b, carry):
        x_core = core[pl.ds(b * WLAT, WLAT)].astype(F32).reshape(WLAT * cols, width).astype(BF16)
        x_halo = (
            halo[pl.ds(b * WLAT, WLAT)].astype(F32).reshape(WLAT * 2 * TILE, width).astype(BF16)
        )
        x_all = jnp.concatenate([x_core, x_halo], axis=0)
        query = directions(dot(x_core, w_qkv[:, :width]), blocks_of, fine_row)
        keys = directions(dot(x_all, w_qkv[:, width : 2 * width]), blocks_of, None)
        values = dot(x_all, w_qkv[:, 2 * width :]).astype(BF16)
        q_code, k_code = q_win * 4, k_win * 4
        for w in range(cols // WLON + 1):
            column = lax.rem(lon * (cols // WLON) + w - 1 + per_row, per_row)
            pattern = window_mask[lat * (rows // WLAT) + b, column]
            by_lat, by_lon = (pattern & 1) * 2, (pattern >> 1) & 1
            q_code = q_code + jnp.where(q_win == w, q_lat * by_lat + q_lon * by_lon, 0)
            k_code = k_code + jnp.where(k_win == w, k_lat * by_lat + k_lon * by_lon, 0)
        no_north = (lat == 0) & (b == 0)
        no_south = (lat == lat_count - 1) & (b == bands - 1)
        gone_low = jnp.where(no_north, 1, 0)
        gone_high = jnp.where(no_south, 1, 0)
        gone = (1 - k_lat) * gone_low + k_lat * gone_high
        k_code = jnp.where((gone > 0) | (k_win < 0), -1, k_code)
        allowed = jnp.where(q_code == k_code, 1.0, 0.0).astype(F32)
        mix[b] = attend(query, keys, values, allowed)
        return carry

    lax.fori_loop(0, bands, band_step, 0)

    for load in loads[5:]:
        load.wait()
    chunk = 2 * WLAT
    size = chunk * cols
    merged_in = []
    flat = mix[...].reshape(bands * WLAT * cols, width)
    for c in range(rows // chunk):
        start = half * cols + c * size
        x = core[pl.ds(half + c * chunk, chunk)].astype(F32).reshape(size, width)
        projected = dot(flat[start : start + size].astype(BF16), w_proj[...])
        result = x + normed(projected)
        out_buf[pl.ds(c * chunk, chunk)] = result.reshape(chunk, blocks, TILE, width).astype(BF16)
        moved = dot(perm[...], result.astype(BF16))
        quarter = size // 4
        quads = jnp.concatenate(
            [moved[g * quarter : (g + 1) * quarter] for g in range(4)], axis=1
        )
        merged_in.append(normed(quads))
    fine_copy = pltpu.make_async_copy(out_buf, fine_out, out_sem)
    fine_copy.start()
    merge_in = jnp.concatenate(merged_in, axis=0).astype(BF16)
    merged = dot(merge_in, w_merge[...]).astype(BF16)
    mid_width = mid_proj.shape[0]
    act = dot(merged, w_mqkv[...])
    mid_row = scale_lanes(mid_scale, mid_width // HEAD)
    query = directions(act[:, :mid_width], blocks_of, mid_row)
    keys = directions(act[:, mid_width : 2 * mid_width], blocks_of, None)
    values = act[:, 2 * mid_width :].astype(BF16)
    allowed = jnp.where(mid_q[...] == mid_k[...], 1.0, 0.0).astype(F32)
    mid_mix = attend(query, keys, values, allowed).astype(BF16)
    mid_result = (merged.astype(F32) + normed(dot(mid_mix, w_mproj[...]))).astype(BF16)
    wide = dot(spread[...], mid_result).reshape(rows // 2, 2 * TILE, mid_result.shape[1])
    mid_out[...] = wide[:, : cols // 2].astype(BF16)
    fine_copy.wait()


def statics(rows, cols):
    half_lat, half_lon = WLAT // 2, WLON // 2
    i, c = np.divmod(np.arange(WLAT * cols), cols)
    core = np.stack(
        [(c + half_lon) // WLON, i >= half_lat, (c + half_lon) % WLON >= half_lon]
    ).astype(np.int32)
    i, m = np.divmod(np.arange(WLAT * 2 * TILE), 2 * TILE)
    west = m < TILE
    real = np.where(west, m >= TILE - half_lon, m < TILE + half_lon)
    window = np.where(west, 0, cols // WLON)
    halo = np.stack([np.where(real, window, -1), i >= half_lat, ~west]).astype(np.int32)
    k_static = np.concatenate([core, halo], axis=1)
    coarse_rows, coarse_cols = rows // 2, cols // 2
    tokens = np.arange(coarse_rows * coarse_cols)
    r, c = np.divmod(tokens, coarse_cols)
    mid = ((r // WLAT) * (coarse_cols // WLON) + c // WLON).astype(np.int32)
    block = np.kron(np.eye(4, dtype=np.float32), np.ones((HEAD, HEAD), np.float32))
    size = 2 * WLAT * cols
    perm = np.zeros((size, size), np.float32)
    out = np.arange(size)
    g, rest = np.divmod(out, size // 4)
    r, s = np.divmod(rest, coarse_cols)
    perm[out, (2 * r + g % 2) * cols + 2 * s + g // 2] = 1.0
    spread = np.zeros((coarse_rows * 2 * TILE, coarse_rows * coarse_cols), np.float32)
    r, c = np.divmod(tokens, coarse_cols)
    spread[r * 2 * TILE + c, tokens] = 1.0
    return (
        jnp.asarray(core.T),
        jnp.asarray(k_static),
        jnp.asarray(mid[:, None]),
        jnp.asarray(mid[None, :]),
        jnp.asarray(block, BF16),
        jnp.asarray(perm, BF16),
        jnp.asarray(spread, BF16),
    )


def per_device(
    lat_count,
    lon_count,
    fine_tokens,
    fine_qkv,
    fine_scale,
    fine_proj,
    window_mask,
    merge_weight,
    mid_qkv,
    mid_scale,
    mid_proj,
):
    rows, cols, width = fine_tokens.shape
    blocks = cols // TILE
    tokens = fine_tokens.reshape(rows, blocks, TILE, width)
    side, latr = exchange(tokens, lat_count, lon_count)
    smem = pl.BlockSpec(memory_space=pltpu.SMEM)
    vmem = pl.BlockSpec(memory_space=pltpu.VMEM)
    anywhere = pl.BlockSpec(memory_space=pl.ANY)
    weights = (fine_qkv, fine_proj, merge_weight, mid_qkv, mid_proj)
    bands = (rows + WLAT) // WLAT
    fine_out, mid_out = pl.pallas_call(
        functools.partial(body_kernel, lat_count),
        out_shape=(
            jax.ShapeDtypeStruct(tokens.shape, BF16),
            jax.ShapeDtypeStruct((rows // 2, cols // 2, merge_weight.shape[1]), BF16),
        ),
        in_specs=[smem] * 3 + [vmem] * 7 + [anywhere] * 8,
        out_specs=(anywhere, vmem),
        scratch_shapes=[
            pltpu.VMEM((rows + WLAT,) + tokens.shape[1:], BF16),
            pltpu.VMEM(side.shape, BF16),
        ]
        + [pltpu.VMEM(w.shape, BF16) for w in weights]
        + [
            pltpu.VMEM((bands, WLAT * cols, width), F32),
            pltpu.VMEM(tokens.shape, BF16),
            pltpu.SemaphoreType.DMA((9,)),
            pltpu.SemaphoreType.DMA,
        ],
        compiler_params=pltpu.CompilerParams(vmem_limit_bytes=50 * 1024 * 1024),
    )(
        fine_scale,
        mid_scale,
        window_mask,
        *statics(rows, cols),
        tokens,
        side,
        latr,
        *weights,
    )
    return fine_out.reshape(rows, cols, width), mid_out


def solution(mesh):
    return jax.shard_map(
        functools.partial(per_device, mesh.shape["lat"], mesh.shape["lon"]),
        mesh=mesh,
        in_specs=(P("lat", "lon", None), P(), P(), P(), P(), P(), P(), P(), P()),
        out_specs=(P("lat", "lon", None), P("lat", "lon", None)),
        check_vma=False,
    )
```

```python
import functools
import math

import jax
import jax.numpy as jnp
import numpy as np
from jax import lax
from jax.experimental import pallas as pl
from jax.experimental.pallas import tpu as pltpu
from jax.sharding import PartitionSpec as P

WLAT = 6
WLON = 12
HEAD = 64
TILE = 8
LANES = 128
EPS_NORM = 1e-05
EPS_DIR = 1e-06
LOG2E = math.log2(math.e)
MESH = pl.DeviceIdType.MESH
BF16 = jnp.bfloat16
F32 = jnp.float32


def sends(lat_count, lon_count, tokens, core, halo, send_sem, recv_sem):
    rows, blocks = tokens.shape[0], tokens.shape[1]
    half = WLAT // 2
    lat, lon = lax.axis_index("lat"), lax.axis_index("lon")
    south, north = lax.rem(lat + 1, lat_count), lax.rem(lat + lat_count - 1, lat_count)
    east, west = lax.rem(lon + 1, lon_count), lax.rem(lon + lon_count - 1, lon_count)
    last = blocks - 1
    top, bottom = pl.ds(0, half), pl.ds(rows - half, half)
    below, middle = pl.ds(rows + half, half), pl.ds(half, rows)
    plan = [
        ((lat, east), tokens.at[:, last], halo.at[middle, 0]),
        ((lat, west), tokens.at[:, 0], halo.at[middle, 1]),
        ((south, lon), tokens.at[bottom], core.at[top]),
        ((north, lon), tokens.at[top], core.at[below]),
        ((south, east), tokens.at[bottom, last], halo.at[top, 0]),
        ((north, east), tokens.at[top, last], halo.at[below, 0]),
        ((south, west), tokens.at[bottom, 0], halo.at[top, 1]),
        ((north, west), tokens.at[top, 0], halo.at[below, 1]),
    ]
    return [
        (
            {"lat": to_lat, "lon": to_lon},
            pltpu.make_async_remote_copy(
                src_ref=src,
                dst_ref=dst,
                send_sem=send_sem.at[n],
                recv_sem=recv_sem.at[n],
                device_id={"lat": to_lat, "lon": to_lon},
                device_id_type=MESH,
            ),
        )
        for n, ((to_lat, to_lon), src, dst) in enumerate(plan)
    ]


def normed(values):
    mean = jnp.mean(values, axis=-1, keepdims=True)
    centred = values - mean
    var = jnp.mean(centred * centred, axis=-1, keepdims=True)
    return centred * lax.rsqrt(var + EPS_NORM)


def dot(a, b):
    return jnp.dot(a, b, preferred_element_type=F32)


def directions(values, ones_block, scale_row):
    held = values.astype(BF16).astype(F32)
    squares = (held * held).astype(BF16)
    block = ones_block.shape[0]
    sums = jnp.concatenate(
        [dot(squares[:, s : s + block], ones_block) for s in range(0, values.shape[1], block)],
        axis=1,
    )
    unit = held * lax.rsqrt(sums + EPS_DIR)
    if scale_row is not None:
        unit = unit * scale_row
    return unit.astype(BF16)


def scale_lanes(scale, heads):
    lane = lax.broadcasted_iota(jnp.int32, (1, LANES), 1)
    return jnp.concatenate(
        [
            jnp.where(lane < HEAD, scale[h] * LOG2E, scale[h + 1] * LOG2E)
            for h in range(0, heads, 2)
        ],
        axis=1,
    )


def attend(query, keys, values, allowed):
    count = query.shape[0]
    lane = lax.broadcasted_iota(jnp.int32, (1, LANES), 1)
    low = (lane < HEAD).astype(F32).astype(BF16)
    high = (lane >= HEAD).astype(F32).astype(BF16)
    first = jnp.broadcast_to(lane < HEAD, (count, LANES))
    ones = jnp.ones((keys.shape[0], LANES), BF16)
    both = jnp.concatenate([allowed, allowed], axis=0)
    mixed = []
    for s in range(0, query.shape[1], LANES):
        pair = query[:, s : s + LANES]
        stacked = jnp.concatenate([pair * low, pair * high], axis=0)
        score = lax.dot_general(
            stacked, keys[:, s : s + LANES], (((1,), (1,)), ((), ())), preferred_element_type=F32
        )
        expo = (jnp.exp2(score) * both).astype(BF16)
        out = dot(expo, jnp.concatenate([values[:, s : s + LANES], ones], axis=1))
        top = jnp.where(first, out[:count, :LANES], out[count:, :LANES])
        total = jnp.where(first, out[:count, LANES:], out[count:, LANES:])
        mixed.append(top / total)
    return jnp.concatenate(mixed, axis=1)


def body_kernel(
    lat_count,
    lon_count,
    fine_scale,
    mid_scale,
    window_mask,
    q_static_hbm,
    k_static_hbm,
    mid_q_hbm,
    mid_k_hbm,
    block_hbm,
    perm_hbm,
    spread_hbm,
    tokens,
    fine_qkv,
    fine_proj,
    merge_weight,
    mid_qkv,
    mid_proj,
    fine_out,
    mid_out,
    core,
    halo,
    q_static,
    k_static,
    mid_q,
    mid_k,
    ones_block,
    perm,
    spread,
    w_qkv,
    w_proj,
    w_merge,
    w_mqkv,
    w_mproj,
    q_s,
    k_s,
    v_s,
    mix,
    out_buf,
    sem,
    out_sem,
    send_sem,
    recv_sem,
):
    rows, blocks, _, width = tokens.shape
    half = WLAT // 2
    cols = blocks * TILE
    bands = (rows + WLAT) // WLAT
    place = WLAT * cols
    beside = WLAT * 2 * TILE
    copies = sends(lat_count, lon_count, tokens, core, halo, send_sem, recv_sem)
    barrier = pltpu.get_barrier_semaphore()
    for device, _ in copies:
        pl.semaphore_signal(barrier, inc=1, device_id=device, device_id_type=MESH)
    loads = [
        pltpu.make_async_copy(src, dst, sem.at[n])
        for n, (src, dst) in enumerate(
            [
                (tokens, core.at[pl.ds(half, rows)]),
                (fine_qkv, w_qkv),
                (block_hbm, ones_block),
                (q_static_hbm, q_static),
                (k_static_hbm, k_static),
                (fine_proj, w_proj),
                (perm_hbm, perm),
                (merge_weight, w_merge),
                (mid_qkv, w_mqkv),
                (mid_q_hbm, mid_q),
                (mid_k_hbm, mid_k),
                (mid_proj, w_mproj),
                (spread_hbm, spread),
            ]
        )
    ]
    for load in loads:
        load.start()
    pl.semaphore_wait(barrier, len(copies))
    for _, copy in copies:
        copy.start()
    lat, lon = lax.axis_index("lat"), lax.axis_index("lon")
    fine_row = scale_lanes(fine_scale, width // HEAD)
    for load in loads[:5]:
        load.wait()
    blocks_of = ones_block[...].astype(BF16)

    def rows_of(ref, first, count):
        part = ref[pl.ds(first, count)]
        return part.astype(F32).reshape(part.shape[0] * part.shape[1] * TILE, width).astype(BF16)

    def query_of(x):
        return directions(dot(x, w_qkv[:, :width]), blocks_of, fine_row)

    def keys_of(x):
        return directions(dot(x, w_qkv[:, width : 2 * width]), blocks_of, None)

    def values_of(x):
        return dot(x, w_qkv[:, 2 * width :]).astype(BF16)

    inner = bands - 2
    own = rows_of(core, WLAT, inner * WLAT)
    q_s[pl.ds(1, inner)] = query_of(own).reshape(inner, place, width)
    k_s[pl.ds(1, inner), pl.ds(0, place)] = keys_of(own).reshape(inner, place, width)
    v_s[pl.ds(1, inner), pl.ds(0, place)] = values_of(own).reshape(inner, place, width)
    for _, copy in copies:
        copy.wait_recv()
    ends = jnp.concatenate(
        [rows_of(core, 0, WLAT), rows_of(core, rows, WLAT), rows_of(halo, 0, rows + WLAT)], axis=0
    )
    query = query_of(ends[: 2 * place])
    for target, found in ((k_s, keys_of(ends)), (v_s, values_of(ends))):
        target[0, pl.ds(0, place)] = found[:place]
        target[bands - 1, pl.ds(0, place)] = found[place : 2 * place]
        target[:, pl.ds(place, beside)] = found[2 * place :].reshape(bands, beside, width)
    q_s[0] = query[:place]
    q_s[bands - 1] = query[place:]
    q_win, q_lat, q_lon = q_static[:, 0:1], q_static[:, 1:2], q_static[:, 2:3]
    k_win, k_lat, k_lon = k_static[0:1], k_static[1:2], k_static[2:3]
    per_row = window_mask.shape[1]

    def band_step(b, carry):
        q_code, k_code = q_win * 4, k_win * 4
        for w in range(cols // WLON + 1):
            column = lax.rem(lon * (cols // WLON) + w - 1 + per_row, per_row)
            pattern = window_mask[lat * (rows // WLAT) + b, column]
            by_lat, by_lon = (pattern & 1) * 2, (pattern >> 1) & 1
            q_code = q_code + jnp.where(q_win == w, q_lat * by_lat + q_lon * by_lon, 0)
            k_code = k_code + jnp.where(k_win == w, k_lat * by_lat + k_lon * by_lon, 0)
        no_north = (lat == 0) & (b == 0)
        no_south = (lat == lat_count - 1) & (b == bands - 1)
        gone_low = jnp.where(no_north, 1, 0)
        gone_high = jnp.where(no_south, 1, 0)
        gone = (1 - k_lat) * gone_low + k_lat * gone_high
        k_code = jnp.where((gone > 0) | (k_win < 0), -1, k_code)
        allowed = jnp.where(q_code == k_code, 1.0, 0.0).astype(F32)
        mix[b] = attend(q_s[b], k_s[b], v_s[b], allowed)
        return carry

    lax.fori_loop(0, bands, band_step, 0)

    for load in loads[5:]:
        load.wait()
    mover = perm[...].astype(BF16)
    chunk = 2 * WLAT
    size = chunk * cols
    merged_in = []
    flat = mix[...].reshape(bands * WLAT * cols, width)
    for c in range(rows // chunk):
        start = half * cols + c * size
        x = core[pl.ds(half + c * chunk, chunk)].astype(F32).reshape(size, width)
        projected = dot(flat[start : start + size].astype(BF16), w_proj[...])
        result = x + normed(projected)
        out_buf[pl.ds(c * chunk, chunk)] = result.reshape(chunk, blocks, TILE, width).astype(BF16)
        moved = dot(mover, result.astype(BF16))
        quarter = size // 4
        quads = jnp.concatenate(
            [moved[g * quarter : (g + 1) * quarter] for g in range(4)], axis=1
        )
        merged_in.append(normed(quads))
    fine_copy = pltpu.make_async_copy(out_buf, fine_out, out_sem)
    fine_copy.start()
    merge_in = jnp.concatenate(merged_in, axis=0).astype(BF16)
    merged = dot(merge_in, w_merge[...]).astype(BF16)
    mid_width = mid_proj.shape[0]
    act = dot(merged, w_mqkv[...])
    mid_row = scale_lanes(mid_scale, mid_width // HEAD)
    query = directions(act[:, :mid_width], blocks_of, mid_row)
    keys = directions(act[:, mid_width : 2 * mid_width], blocks_of, None)
    values = act[:, 2 * mid_width :].astype(BF16)
    allowed = jnp.where(mid_q[...] == mid_k[...], 1.0, 0.0).astype(F32)
    mid_mix = attend(query, keys, values, allowed).astype(BF16)
    mid_result = (merged.astype(F32) + normed(dot(mid_mix, w_mproj[...]))).astype(BF16)
    wide = dot(spread[...].astype(BF16), mid_result).reshape(rows // 2, 2 * TILE, mid_result.shape[1])
    mid_out[...] = wide[:, : cols // 2].astype(BF16)
    fine_copy.wait()
    for _, copy in copies:
        copy.wait_send()


def statics(rows, cols):
    half_lat, half_lon = WLAT // 2, WLON // 2
    i, c = np.divmod(np.arange(WLAT * cols), cols)
    core = np.stack(
        [(c + half_lon) // WLON, i >= half_lat, (c + half_lon) % WLON >= half_lon]
    ).astype(np.int32)
    i, m = np.divmod(np.arange(WLAT * 2 * TILE), 2 * TILE)
    west = m < TILE
    real = np.where(west, m >= TILE - half_lon, m < TILE + half_lon)
    window = np.where(west, 0, cols // WLON)
    halo = np.stack([np.where(real, window, -1), i >= half_lat, ~west]).astype(np.int32)
    k_static = np.concatenate([core, halo], axis=1)
    coarse_rows, coarse_cols = rows // 2, cols // 2
    tokens = np.arange(coarse_rows * coarse_cols)
    r, c = np.divmod(tokens, coarse_cols)
    mid = ((r // WLAT) * (coarse_cols // WLON) + c // WLON).astype(np.int32)
    block = np.kron(np.eye(4, dtype=np.float32), np.ones((HEAD, HEAD), np.float32))
    size = 2 * WLAT * cols
    perm = np.zeros((size, size), np.float32)
    out = np.arange(size)
    g, rest = np.divmod(out, size // 4)
    r, s = np.divmod(rest, coarse_cols)
    perm[out, (2 * r + g % 2) * cols + 2 * s + g // 2] = 1.0
    spread = np.zeros((coarse_rows * 2 * TILE, coarse_rows * coarse_cols), np.float32)
    r, c = np.divmod(tokens, coarse_cols)
    spread[r * 2 * TILE + c, tokens] = 1.0
    return (
        jnp.asarray(core.T),
        jnp.asarray(k_static),
        jnp.asarray(mid[:, None]),
        jnp.asarray(mid[None, :]),
        jnp.asarray(block),
        jnp.asarray(perm),
        jnp.asarray(spread),
    )


def per_device(
    lat_count,
    lon_count,
    fine_tokens,
    fine_qkv,
    fine_scale,
    fine_proj,
    window_mask,
    merge_weight,
    mid_qkv,
    mid_scale,
    mid_proj,
):
    rows, cols, width = fine_tokens.shape
    blocks = cols // TILE
    tokens = fine_tokens.reshape(rows, blocks, TILE, width)
    smem = pl.BlockSpec(memory_space=pltpu.SMEM)
    vmem = pl.BlockSpec(memory_space=pltpu.VMEM)
    anywhere = pl.BlockSpec(memory_space=pl.ANY)
    weights = (fine_qkv, fine_proj, merge_weight, mid_qkv, mid_proj)
    tables = statics(rows, cols)
    bands = (rows + WLAT) // WLAT
    reach = WLAT * (cols + 2 * TILE)
    fine_out, mid_out = pl.pallas_call(
        functools.partial(body_kernel, lat_count, lon_count),
        out_shape=(
            jax.ShapeDtypeStruct(tokens.shape, BF16),
            jax.ShapeDtypeStruct((rows // 2, cols // 2, merge_weight.shape[1]), BF16),
        ),
        in_specs=[smem] * 3 + [anywhere] * 13,
        out_specs=(anywhere, vmem),
        scratch_shapes=[
            pltpu.VMEM((rows + WLAT,) + tokens.shape[1:], BF16),
            pltpu.VMEM((rows + WLAT, 2, TILE, width), BF16),
        ]
        + [pltpu.VMEM(t.shape, t.dtype) for t in tables]
        + [pltpu.VMEM(w.shape, BF16) for w in weights]
        + [
            pltpu.VMEM((bands, WLAT * cols, width), BF16),
            pltpu.VMEM((bands, reach, width), BF16),
            pltpu.VMEM((bands, reach, width), BF16),
            pltpu.VMEM((bands, WLAT * cols, width), F32),
            pltpu.VMEM(tokens.shape, BF16),
            pltpu.SemaphoreType.DMA((13,)),
            pltpu.SemaphoreType.DMA,
            pltpu.SemaphoreType.DMA((8,)),
            pltpu.SemaphoreType.DMA((8,)),
        ],
        compiler_params=pltpu.CompilerParams(
            collective_id=0, has_side_effects=True, vmem_limit_bytes=60 * 1024 * 1024
        ),
    )(
        fine_scale,
        mid_scale,
        window_mask,
        *tables,
        tokens,
        *weights,
    )
    return fine_out.reshape(rows, cols, width), mid_out


def solution(mesh):
    return jax.shard_map(
        functools.partial(per_device, mesh.shape["lat"], mesh.shape["lon"]),
        mesh=mesh,
        in_specs=(P("lat", "lon", None), P(), P(), P(), P(), P(), P(), P(), P()),
        out_specs=(P("lat", "lon", None), P("lat", "lon", None)),
        check_vma=False,
    )
```

```python
import functools
import math

import jax
import jax.numpy as jnp
import numpy as np
from jax import lax
from jax.experimental import pallas as pl
from jax.experimental.pallas import tpu as pltpu
from jax.sharding import PartitionSpec as P

WLAT = 6
WLON = 12
HEAD = 64
TILE = 8
LANES = 128
EPS_NORM = 1e-05
EPS_DIR = 1e-06
LOG2E = math.log2(math.e)
MESH = pl.DeviceIdType.MESH
BF16 = jnp.bfloat16
F32 = jnp.float32


def sends(lat_count, lon_count, tokens, core, halo, send_sem, recv_sem):
    rows, blocks = tokens.shape[0], tokens.shape[1]
    half = WLAT // 2
    lat, lon = lax.axis_index("lat"), lax.axis_index("lon")
    south, north = lax.rem(lat + 1, lat_count), lax.rem(lat + lat_count - 1, lat_count)
    east, west = lax.rem(lon + 1, lon_count), lax.rem(lon + lon_count - 1, lon_count)
    last = blocks - 1
    top, bottom = pl.ds(0, half), pl.ds(rows - half, half)
    below, middle = pl.ds(rows + half, half), pl.ds(half, rows)
    plan = [
        ((lat, east), tokens.at[:, last], halo.at[middle, 0]),
        ((lat, west), tokens.at[:, 0], halo.at[middle, 1]),
        ((south, lon), tokens.at[bottom], core.at[top]),
        ((north, lon), tokens.at[top], core.at[below]),
        ((south, east), tokens.at[bottom, last], halo.at[top, 0]),
        ((north, east), tokens.at[top, last], halo.at[below, 0]),
        ((south, west), tokens.at[bottom, 0], halo.at[top, 1]),
        ((north, west), tokens.at[top, 0], halo.at[below, 1]),
    ]
    return [
        (
            {"lat": to_lat, "lon": to_lon},
            pltpu.make_async_remote_copy(
                src_ref=src,
                dst_ref=dst,
                send_sem=send_sem.at[n],
                recv_sem=recv_sem.at[n],
                device_id={"lat": to_lat, "lon": to_lon},
                device_id_type=MESH,
            ),
        )
        for n, ((to_lat, to_lon), src, dst) in enumerate(plan)
    ]


def normed(values):
    mean = jnp.mean(values, axis=-1, keepdims=True)
    centred = values - mean
    var = jnp.mean(centred * centred, axis=-1, keepdims=True)
    return centred * lax.rsqrt(var + EPS_NORM)


def dot(a, b):
    return jnp.dot(a, b, preferred_element_type=F32)


def directions(values, ones_block, scale_row):
    held = values.astype(BF16).astype(F32)
    squares = (held * held).astype(BF16)
    block = ones_block.shape[0]
    sums = jnp.concatenate(
        [dot(squares[:, s : s + block], ones_block) for s in range(0, values.shape[1], block)],
        axis=1,
    )
    unit = held * lax.rsqrt(sums + EPS_DIR)
    if scale_row is not None:
        unit = unit * scale_row
    return unit.astype(BF16)


def scale_lanes(scale, heads):
    lane = lax.broadcasted_iota(jnp.int32, (1, LANES), 1)
    return jnp.concatenate(
        [
            jnp.where(lane < HEAD, scale[h] * LOG2E, scale[h + 1] * LOG2E)
            for h in range(0, heads, 2)
        ],
        axis=1,
    )


def attend(query, keys, values, allowed):
    count = query.shape[0]
    lane = lax.broadcasted_iota(jnp.int32, (1, LANES), 1)
    low = (lane < HEAD).astype(F32).astype(BF16)
    high = (lane >= HEAD).astype(F32).astype(BF16)
    first = jnp.broadcast_to(lane < HEAD, (count, LANES))
    ones = jnp.ones((keys.shape[0], LANES), BF16)
    both = jnp.concatenate([allowed, allowed], axis=0)
    mixed = []
    for s in range(0, query.shape[1], LANES):
        pair = query[:, s : s + LANES]
        stacked = jnp.concatenate([pair * low, pair * high], axis=0)
        score = lax.dot_general(
            stacked, keys[:, s : s + LANES], (((1,), (1,)), ((), ())), preferred_element_type=F32
        )
        expo = (jnp.exp2(score) * both).astype(BF16)
        out = dot(expo, jnp.concatenate([values[:, s : s + LANES], ones], axis=1))
        top = jnp.where(first, out[:count, :LANES], out[count:, :LANES])
        total = jnp.where(first, out[:count, LANES:], out[count:, LANES:])
        mixed.append(top / total)
    return jnp.concatenate(mixed, axis=1)


def attention_kernel(
    lat_count,
    lon_count,
    fine_scale,
    window_mask,
    q_static_hbm,
    k_static_hbm,
    block_hbm,
    tokens,
    fine_qkv,
    mix_out,
    core,
    halo,
    q_static,
    k_static,
    ones_block,
    w_qkv,
    q_s,
    k_s,
    v_s,
    mix,
    sem,
    out_sem,
    send_sem,
    recv_sem,
):
    rows, blocks, _, width = tokens.shape
    half = WLAT // 2
    cols = blocks * TILE
    bands = (rows + WLAT) // WLAT
    place = WLAT * cols
    beside = WLAT * 2 * TILE
    copies = sends(lat_count, lon_count, tokens, core, halo, send_sem, recv_sem)
    barrier = pltpu.get_barrier_semaphore()
    for device, _ in copies:
        pl.semaphore_signal(barrier, inc=1, device_id=device, device_id_type=MESH)
    loads = [
        pltpu.make_async_copy(src, dst, sem.at[n])
        for n, (src, dst) in enumerate(
            [
                (tokens, core.at[pl.ds(half, rows)]),
                (fine_qkv, w_qkv),
                (block_hbm, ones_block),
                (q_static_hbm, q_static),
                (k_static_hbm, k_static),
            ]
        )
    ]
    for load in loads:
        load.start()
    pl.semaphore_wait(barrier, len(copies))
    for _, copy in copies:
        copy.start()
    lat, lon = lax.axis_index("lat"), lax.axis_index("lon")
    fine_row = scale_lanes(fine_scale, width // HEAD)
    for load in loads:
        load.wait()
    blocks_of = ones_block[...].astype(BF16)

    def rows_of(ref, first, count):
        part = ref[pl.ds(first, count)]
        return part.astype(F32).reshape(part.shape[0] * part.shape[1] * TILE, width).astype(BF16)

    def query_of(x):
        return directions(dot(x, w_qkv[:, :width]), blocks_of, fine_row)

    def keys_of(x):
        return directions(dot(x, w_qkv[:, width : 2 * width]), blocks_of, None)

    def values_of(x):
        return dot(x, w_qkv[:, 2 * width :]).astype(BF16)

    inner = bands - 2
    own = rows_of(core, WLAT, inner * WLAT)
    q_s[pl.ds(1, inner)] = query_of(own).reshape(inner, place, width)
    k_s[pl.ds(1, inner), pl.ds(0, place)] = keys_of(own).reshape(inner, place, width)
    v_s[pl.ds(1, inner), pl.ds(0, place)] = values_of(own).reshape(inner, place, width)
    for _, copy in copies:
        copy.wait_recv()
    ends = jnp.concatenate(
        [rows_of(core, 0, WLAT), rows_of(core, rows, WLAT), rows_of(halo, 0, rows + WLAT)], axis=0
    )
    query = query_of(ends[: 2 * place])
    for target, found in ((k_s, keys_of(ends)), (v_s, values_of(ends))):
        target[0, pl.ds(0, place)] = found[:place]
        target[bands - 1, pl.ds(0, place)] = found[place : 2 * place]
        target[:, pl.ds(place, beside)] = found[2 * place :].reshape(bands, beside, width)
    q_s[0] = query[:place]
    q_s[bands - 1] = query[place:]
    q_win, q_lat, q_lon = q_static[:, 0:1], q_static[:, 1:2], q_static[:, 2:3]
    k_win, k_lat, k_lon = k_static[0:1], k_static[1:2], k_static[2:3]
    per_row = window_mask.shape[1]

    written = []
    for b in range(bands):
        q_code, k_code = q_win * 4, k_win * 4
        for w in range(cols // WLON + 1):
            column = lax.rem(lon * (cols // WLON) + w - 1 + per_row, per_row)
            pattern = window_mask[lat * (rows // WLAT) + b, column]
            by_lat, by_lon = (pattern & 1) * 2, (pattern >> 1) & 1
            q_code = q_code + jnp.where(q_win == w, q_lat * by_lat + q_lon * by_lon, 0)
            k_code = k_code + jnp.where(k_win == w, k_lat * by_lat + k_lon * by_lon, 0)
        no_north = (lat == 0) if b == 0 else False
        no_south = (lat == lat_count - 1) if b == bands - 1 else False
        gone_low = jnp.where(no_north, 1, 0)
        gone_high = jnp.where(no_south, 1, 0)
        gone = (1 - k_lat) * gone_low + k_lat * gone_high
        k_code = jnp.where((gone > 0) | (k_win < 0), -1, k_code)
        allowed = jnp.where(q_code == k_code, 1.0, 0.0).astype(F32)
        mix[b] = attend(q_s[b], k_s[b], v_s[b], allowed).astype(BF16)
        write = pltpu.make_async_copy(mix.at[b], mix_out.at[b], out_sem.at[b])
        write.start()
        written.append(write)
    for write in written:
        write.wait()
    for _, copy in copies:
        copy.wait_send()


def tail_kernel(
    mid_scale,
    mix_hbm,
    tokens,
    fine_proj,
    perm_hbm,
    merge_weight,
    mid_qkv,
    block_hbm,
    mid_q_hbm,
    mid_k_hbm,
    mid_proj,
    spread_hbm,
    fine_out,
    mid_out,
    mix,
    core,
    w_proj,
    perm,
    w_merge,
    w_mqkv,
    ones_block,
    mid_q,
    mid_k,
    w_mproj,
    spread,
    out_buf,
    sem,
    out_sem,
):
    rows, blocks, _, width = tokens.shape
    half = WLAT // 2
    cols = blocks * TILE
    bands = (rows + WLAT) // WLAT
    loads = [
        pltpu.make_async_copy(src, dst, sem.at[n])
        for n, (src, dst) in enumerate(
            [
                (mix_hbm, mix),
                (tokens, core),
                (fine_proj, w_proj),
                (perm_hbm, perm),
                (merge_weight, w_merge),
                (mid_qkv, w_mqkv),
                (block_hbm, ones_block),
                (mid_q_hbm, mid_q),
                (mid_k_hbm, mid_k),
                (mid_proj, w_mproj),
                (spread_hbm, spread),
            ]
        )
    ]
    for load in loads:
        load.start()
    for load in loads[:4]:
        load.wait()
    mover = perm[...].astype(BF16)
    chunk = 2 * WLAT
    size = chunk * cols
    merged_in = []
    flat = mix[...].astype(F32).reshape(bands * WLAT * cols, width)
    for c in range(rows // chunk):
        start = half * cols + c * size
        x = core[pl.ds(c * chunk, chunk)].astype(F32).reshape(size, width)
        projected = dot(flat[start : start + size].astype(BF16), w_proj[...])
        result = x + normed(projected)
        out_buf[pl.ds(c * chunk, chunk)] = result.reshape(chunk, blocks, TILE, width).astype(BF16)
        moved = dot(mover, result.astype(BF16))
        quarter = size // 4
        quads = jnp.concatenate(
            [moved[g * quarter : (g + 1) * quarter] for g in range(4)], axis=1
        )
        merged_in.append(normed(quads))
    fine_copy = pltpu.make_async_copy(out_buf, fine_out, out_sem)
    fine_copy.start()
    for load in loads[4:]:
        load.wait()
    blocks_of = ones_block[...].astype(BF16)
    merge_in = jnp.concatenate(merged_in, axis=0).astype(BF16)
    merged = dot(merge_in, w_merge[...]).astype(BF16)
    mid_width = mid_proj.shape[0]
    act = dot(merged, w_mqkv[...])
    mid_row = scale_lanes(mid_scale, mid_width // HEAD)
    query = directions(act[:, :mid_width], blocks_of, mid_row)
    keys = directions(act[:, mid_width : 2 * mid_width], blocks_of, None)
    values = act[:, 2 * mid_width :].astype(BF16)
    allowed = jnp.where(mid_q[...] == mid_k[...], 1.0, 0.0).astype(F32)
    mid_mix = attend(query, keys, values, allowed).astype(BF16)
    mid_result = (merged.astype(F32) + normed(dot(mid_mix, w_mproj[...]))).astype(BF16)
    wide = dot(spread[...].astype(BF16), mid_result).reshape(rows // 2, 2 * TILE, mid_result.shape[1])
    mid_out[...] = wide[:, : cols // 2].astype(BF16)
    fine_copy.wait()


def statics(rows, cols):
    half_lat, half_lon = WLAT // 2, WLON // 2
    i, c = np.divmod(np.arange(WLAT * cols), cols)
    core = np.stack(
        [(c + half_lon) // WLON, i >= half_lat, (c + half_lon) % WLON >= half_lon]
    ).astype(np.int32)
    i, m = np.divmod(np.arange(WLAT * 2 * TILE), 2 * TILE)
    west = m < TILE
    real = np.where(west, m >= TILE - half_lon, m < TILE + half_lon)
    window = np.where(west, 0, cols // WLON)
    halo = np.stack([np.where(real, window, -1), i >= half_lat, ~west]).astype(np.int32)
    k_static = np.concatenate([core, halo], axis=1)
    coarse_rows, coarse_cols = rows // 2, cols // 2
    tokens = np.arange(coarse_rows * coarse_cols)
    r, c = np.divmod(tokens, coarse_cols)
    mid = ((r // WLAT) * (coarse_cols // WLON) + c // WLON).astype(np.int32)
    block = np.kron(np.eye(4, dtype=np.float32), np.ones((HEAD, HEAD), np.float32))
    size = 2 * WLAT * cols
    perm = np.zeros((size, size), np.float32)
    out = np.arange(size)
    g, rest = np.divmod(out, size // 4)
    r, s = np.divmod(rest, coarse_cols)
    perm[out, (2 * r + g % 2) * cols + 2 * s + g // 2] = 1.0
    spread = np.zeros((coarse_rows * 2 * TILE, coarse_rows * coarse_cols), np.float32)
    r, c = np.divmod(tokens, coarse_cols)
    spread[r * 2 * TILE + c, tokens] = 1.0
    return (
        jnp.asarray(core.T),
        jnp.asarray(k_static),
        jnp.asarray(mid[:, None]),
        jnp.asarray(mid[None, :]),
        jnp.asarray(block),
        jnp.asarray(perm),
        jnp.asarray(spread),
    )


def per_device(
    lat_count,
    lon_count,
    fine_tokens,
    fine_qkv,
    fine_scale,
    fine_proj,
    window_mask,
    merge_weight,
    mid_qkv,
    mid_scale,
    mid_proj,
):
    rows, cols, width = fine_tokens.shape
    blocks = cols // TILE
    tokens = fine_tokens.reshape(rows, blocks, TILE, width)
    smem = pl.BlockSpec(memory_space=pltpu.SMEM)
    vmem = pl.BlockSpec(memory_space=pltpu.VMEM)
    anywhere = pl.BlockSpec(memory_space=pl.ANY)
    q_static, k_static, mid_q, mid_k, block, perm, spread = statics(rows, cols)
    bands = (rows + WLAT) // WLAT
    reach = WLAT * (cols + 2 * TILE)
    held = pltpu.CompilerParams(vmem_limit_bytes=60 * 1024 * 1024)
    first = (q_static, k_static, block, tokens, fine_qkv)
    mix = pl.pallas_call(
        functools.partial(attention_kernel, lat_count, lon_count),
        out_shape=jax.ShapeDtypeStruct((bands, WLAT * cols, width), BF16),
        in_specs=[smem] * 2 + [anywhere] * len(first),
        out_specs=anywhere,
        scratch_shapes=[
            pltpu.VMEM((rows + WLAT,) + tokens.shape[1:], BF16),
            pltpu.VMEM((rows + WLAT, 2, TILE, width), BF16),
            pltpu.VMEM(q_static.shape, q_static.dtype),
            pltpu.VMEM(k_static.shape, k_static.dtype),
            pltpu.VMEM(block.shape, block.dtype),
            pltpu.VMEM(fine_qkv.shape, BF16),
            pltpu.VMEM((bands, WLAT * cols, width), BF16),
            pltpu.VMEM((bands, reach, width), BF16),
            pltpu.VMEM((bands, reach, width), BF16),
            pltpu.VMEM((bands, WLAT * cols, width), BF16),
            pltpu.SemaphoreType.DMA((len(first),)),
            pltpu.SemaphoreType.DMA((bands,)),
            pltpu.SemaphoreType.DMA((8,)),
            pltpu.SemaphoreType.DMA((8,)),
        ],
        compiler_params=pltpu.CompilerParams(
            collective_id=0, has_side_effects=True, vmem_limit_bytes=60 * 1024 * 1024
        ),
    )(fine_scale, window_mask, *first)
    second = (
        mix,
        tokens,
        fine_proj,
        perm,
        merge_weight,
        mid_qkv,
        block,
        mid_q,
        mid_k,
        mid_proj,
        spread,
    )
    fine_out, mid_out = pl.pallas_call(
        tail_kernel,
        out_shape=(
            jax.ShapeDtypeStruct(tokens.shape, BF16),
            jax.ShapeDtypeStruct((rows // 2, cols // 2, merge_weight.shape[1]), BF16),
        ),
        in_specs=[smem] + [anywhere] * len(second),
        out_specs=(anywhere, vmem),
        scratch_shapes=[pltpu.VMEM(a.shape, a.dtype) for a in second]
        + [
            pltpu.VMEM(tokens.shape, BF16),
            pltpu.SemaphoreType.DMA((len(second),)),
            pltpu.SemaphoreType.DMA,
        ],
        compiler_params=held,
    )(mid_scale, *second)
    return fine_out.reshape(rows, cols, width), mid_out


def solution(mesh):
    return jax.shard_map(
        functools.partial(per_device, mesh.shape["lat"], mesh.shape["lon"]),
        mesh=mesh,
        in_specs=(P("lat", "lon", None), P(), P(), P(), P(), P(), P(), P(), P()),
        out_specs=(P("lat", "lon", None), P("lat", "lon", None)),
        check_vma=False,
    )
```
